128 devices in a mesh: lat: 64 (over z, y, x), lev: 2 (over core).
Axes of the slice: x: 4, y: 4, z: 4, core: 2. Of those that a mesh axis runs over, the one named last changes fastest.
Arguments:
- grid_values: bfloat16 [2560, 64, 5136], P('lat', 'lev'), may hold values from -6 to 6
- lat_counts: int32 [1280], P('lat'), may hold values from 8 to 5136, as said below
- wave_table: int32 [128], replicated, may hold values from 0 to 1279, as said below
- inverses: float32 [2560, 2, 32, 32], P('lat'), may hold values from -1 to 1
- legendre: bfloat16 [128, 2, 640, 1280], P('lat', None, 'lev')
Outputs:
- spectral: bfloat16 [128, 2, 640, 128], P('lat', None, 'lev')
The draws below stay inside these ranges and needn't reach their ends.
Inputs may be any that keep to these rules, and one draw needn't show every extreme that they name: `lat_counts`: a multiple of 4 on every pair; 8 on the polar pair, 5136 on the pair nearest the equator, 20 + 4 p less 0 to 12 on pair p between. `wave_table`: distinct wavenumbers; 0 and 1279 are always among them.
All inputs are finite; a program needn't handle non-finite values.
Results may differ from the reference program's by a relative error of at most 0.015.
Values may be sent and summed in bfloat16 or wider, within the bound.
No kernel may reach another device: no remote copies, remote signals or barrier semaphores. Data moves between devices by JAX's collectives and lax.ppermute only.
A program may use at most 128 MiB of HBM per device.

```python
import math
import jax
import jax.numpy as jnp
from jax import lax

TRUNC = 1279
LEV = 32
FIELDS = 2
FL = 64
HALF_DEG = 640
NPAIR = 1280
NLAT = 2560
NLON = 5136
M_FLIGHT = 128


def draw_lat_counts(key, part):
    pair_index = jnp.arange(NPAIR, dtype=jnp.int32)
    trimmed = jax.random.randint(key, (NPAIR,), 0, 4)
    trimmed = jnp.where(pair_index == 0, 3, jnp.where(pair_index == NPAIR - 1, 0, trimmed))
    return (20 + 4 * pair_index - 4 * trimmed).astype(jnp.int32)


def draw_wave_table(key, part):
    inner = jax.random.permutation(jax.random.fold_in(key, 11), TRUNC - 1) + 1
    chosen = inner[:M_FLIGHT - 2].astype(jnp.int32)
    ends = jnp.array([0, TRUNC], dtype=jnp.int32)
    joined = jnp.concatenate([ends, chosen])
    return jax.random.permutation(jax.random.fold_in(key, 12), joined).astype(jnp.int32)


def draw_legendre(key, part):
    pair_index = jnp.arange(NPAIR, dtype=jnp.float32)
    spread = jnp.sqrt(2.0 * (5.0 + pair_index) / NPAIR)
    shape = (M_FLIGHT, 2, HALF_DEG, NPAIR)
    base = jax.random.normal(jax.random.fold_in(key, 23), shape, jnp.float32)
    return (base * spread).astype(jnp.bfloat16)


def block_scale(key, shape, split, least, largest):
    level = 1.0
    for position, shards_of in split:
        draws = jax.random.uniform(jax.random.fold_in(jax.random.fold_in(key, 6), position), (shards_of,), jnp.float32, least / len(split), largest / len(split))
        level = level * jnp.repeat(jnp.exp(draws), shape[position] // shards_of).reshape((-1,) + (1,) * (len(shape) - 1 - position))
    return level


def gaussian(stream_key, shape, scale, limit, pieces=(), kind=jnp.bfloat16):
    values = jax.random.normal(stream_key, shape, jnp.float32) * scale
    if len(pieces) > 0:
        values = block_scale(stream_key, shape, pieces, -0.22, 0.18) * values
    return jnp.clip(values, min=-limit, max=limit).astype(kind)


def setup_inputs(seed: int = 0) -> dict:
    streams_of = jax.random.split(jax.random.key(seed), 6)
    return {
        "grid_values": gaussian(streams_of[0], (NLAT, FL, NLON), 1.0, 6.0, ((0, 64), (1, 2))),
        "lat_counts": draw_lat_counts(jax.random.fold_in(streams_of[5], 71), 0),
        "wave_table": draw_wave_table(jax.random.fold_in(streams_of[5], 71), 0),
        "inverses": gaussian(streams_of[3], (NLAT, FIELDS, LEV, LEV), LEV ** -0.5, 1.0, ((0, 64),), jnp.float32),
        "legendre": draw_legendre(jax.random.fold_in(streams_of[5], 71), 0),
    }


def fourier_table(point_count, wavenumbers, width):
    positions = jnp.arange(width, dtype=jnp.int32)
    phase_index = (positions[:, None] * wavenumbers[None, :]) % point_count
    angles = phase_index.astype(jnp.float32) * (2.0 * math.pi) / point_count.astype(jnp.float32)
    inside = (positions < point_count)[:, None]
    cosines = jnp.where(inside, jnp.cos(angles), 0.0)
    sines = jnp.where(inside, -jnp.sin(angles), 0.0)
    return jnp.concatenate([cosines, sines], axis=1).astype(jnp.bfloat16)


def mix_levels(fourier, inverses):
    band = fourier.shape[0]
    fields = inverses.shape[1]
    levels = inverses.shape[2]
    slots = fourier.shape[3]
    split_data = fourier.astype(jnp.float32).reshape(band, levels, fields, 2, slots)
    mixed = jnp.einsum("aflk,akfrs->sarlf", inverses, split_data, precision=lax.Precision.HIGHEST)
    return mixed.reshape(slots, band, 2, levels * fields)


def reference(grid_values, lat_counts, wave_table, inverses, legendre):
    grouped = grid_values.reshape(NPAIR, 2 * FL, NLON)

    def transform(item):
        pair_rows, point_count = item
        basis = fourier_table(point_count, wave_table, NLON)
        product = jnp.dot(pair_rows, basis, preferred_element_type=jnp.float32)
        product = product / point_count.astype(jnp.float32)
        return product.astype(jnp.bfloat16).reshape(2, FL, 2, M_FLIGHT)

    fourier = lax.map(transform, (grouped, lat_counts)).reshape(NLAT, FL, 2, M_FLIGHT)
    mixed = mix_levels(fourier, inverses)
    paired = mixed.reshape(M_FLIGHT, NPAIR, 2, 2 * FL)
    folded = jnp.stack([paired[:, :, 0] + paired[:, :, 1], paired[:, :, 0] - paired[:, :, 1]], axis=1).astype(jnp.bfloat16)
    steps_index = jnp.arange(HALF_DEG, dtype=jnp.int32)
    parity = jnp.arange(2, dtype=jnp.int32)

    def legendre_sum(item):
        table_slot, folded_slot, wavenumber = item
        summed = jnp.einsum("qjp,qpe->qje", table_slot.astype(jnp.float32), folded_slot.astype(jnp.float32))
        degree = wavenumber + 2 * steps_index[None, :] + parity[:, None]
        keep = (degree <= TRUNC)[:, :, None]
        return jnp.where(keep, summed, 0.0).astype(jnp.bfloat16)

    return lax.map(legendre_sum, (legendre, folded, wave_table))
```

```python
import functools

import jax
import jax.numpy as jnp
from jax import lax
from jax.experimental import pallas as pl
from jax.experimental.pallas import tpu as pltpu
from jax.sharding import PartitionSpec as P

TRUNC = 1279
BLOCK = 256
PAIRS_PER_STEP = 4
MIX_PAIRS = 5
VMEM_LIMIT = 56 * 2**20

COS_TERMS = (1.0, -19.73920440673828, 64.9391098022461, -85.45005798339844,
             60.16698455810547, -25.965150833129883, 6.525190353393555)
SIN_TERMS = (6.2831854820251465, -41.34170150756836, 81.60513305664062, -76.7029800415039,
             42.02566146850586, -14.898837089538574, 3.236703872680664)

f32 = jnp.float32
bf16 = jnp.bfloat16


def horner(z, terms):
    total = jnp.full_like(z, terms[-1])
    for term in terms[-2::-1]:
        total = total * z + term
    return total


def iota(shape, dim):
    return lax.broadcasted_iota(jnp.int32, shape, dim)


def fourier_kernel(counts, waves, grid, out, wave_row, tail):
    step = pl.program_id(0)
    pairs, rows, storage = grid.shape
    blocks = storage // BLOCK
    rest = storage - blocks * BLOCK

    @pl.when(step == 0)
    def _():
        table = jnp.broadcast_to(waves[...], (8, 128))
        order = (iota((128, 128), 0) == (iota((128, 128), 1) % 64) * 2 + iota((128, 128), 1) // 64)
        order = order.astype(f32).astype(bf16)
        high = jnp.dot((table // 64).astype(f32).astype(bf16), order, preferred_element_type=f32)
        low = jnp.dot((table % 64).astype(f32).astype(bf16), order, preferred_element_type=f32)
        wave_row[...] = high * 64.0 + low
        tail[...] = jnp.zeros_like(tail)

    row = iota((40, 128), 0)
    position = jnp.where(row < 16, row, jnp.where(row < 32, (row - 16) * 16, BLOCK)).astype(f32)
    turns = position * wave_row[0:1, :]
    lane = iota((16, BLOCK), 1)
    for i in range(pairs):
        count = counts[step * pairs + i]
        count_f = jnp.full((8, 128), count, jnp.int32).astype(f32)
        inverse = 1.0 / count_f
        inverse5 = jnp.concatenate([inverse] * 5, 0)
        count5 = jnp.concatenate([count_f] * 5, 0)
        whole = jnp.floor(turns * inverse5 + 0.5)
        u = (turns - whole * count5) * inverse5
        z = u * u
        cosine = horner(z, COS_TERMS)
        sine = u * horner(z, SIN_TERMS)
        cos_fine, sin_fine = cosine[0:16], sine[0:16]
        cos_part, sin_part = [], []
        for a in range(16):
            c, s = cosine[16 + a:17 + a], sine[16 + a:17 + a]
            cos_part.append(c * cos_fine - s * sin_fine)
            sin_part.append(-(s * cos_fine + c * sin_fine))
        basis = jnp.concatenate(
            [jnp.concatenate(cos_part, 0), jnp.concatenate(sin_part, 0)], 1
        ).astype(bf16)
        turn_r, turn_i = cosine[32:33], -sine[32:33]
        tail[i, :, 0:rest] = grid[i, :, blocks * BLOCK:storage]
        pieces = []
        for b in range(blocks + 1):
            piece = grid[i, :, b * BLOCK:(b + 1) * BLOCK] if b < blocks else tail[i]
            inside = jnp.where(lane + b * BLOCK < count, 1.0, 0.0).astype(bf16)
            pieces.append(piece * jnp.concatenate([inside] * (rows // 16), 0))
        product = jnp.dot(jnp.concatenate(pieces, 0), basis, preferred_element_type=f32)
        real = imag = None
        for b in range(blocks, -1, -1):
            new_r = product[b * rows:(b + 1) * rows, :128]
            new_i = product[b * rows:(b + 1) * rows, 128:]
            if real is None:
                real, imag = new_r, new_i
            else:
                real, imag = (
                    real * turn_r - imag * turn_i + new_r,
                    real * turn_i + imag * turn_r + new_i,
                )
        scale = inverse[0:1]
        out[i] = jnp.concatenate([real * scale, imag * scale], 1).astype(bf16)


def fourier(grouped, lat_counts, wave_table):
    pair_total, rows, storage = grouped.shape
    step = PAIRS_PER_STEP
    return pl.pallas_call(
        fourier_kernel,
        out_shape=jax.ShapeDtypeStruct((pair_total, rows, 256), bf16),
        grid=(pair_total // step,),
        in_specs=[
            pl.BlockSpec(memory_space=pltpu.SMEM),
            pl.BlockSpec((1, 128), lambda i: (0, 0)),
            pl.BlockSpec((step, rows, storage), lambda i: (i, 0, 0)),
        ],
        out_specs=pl.BlockSpec((step, rows, 256), lambda i: (i, 0, 0)),
        scratch_shapes=[pltpu.VMEM((8, 128), f32), pltpu.VMEM((step, rows, BLOCK), bf16)],
        compiler_params=pltpu.CompilerParams(vmem_limit_bytes=VMEM_LIMIT),
        name="fourier",
    )(lat_counts, wave_table.reshape(1, 128), grouped)


def mix_kernel(inverses, own, other, out, rows_out):
    step = pl.program_id(0)
    slab = lax.axis_index("lev")
    pairs = own.shape[0]
    spread_level = iota((32, 128), 0)
    spread_lane = iota((32, 128), 1)
    level = (((spread_lane >> 5) & 1) ^ slab) * 16 + ((spread_lane >> 1) & 15)
    spread = (spread_level == level).astype(f32).astype(bf16)
    matrices = jnp.dot(inverses[...], spread, preferred_element_type=f32)
    row = iota(matrices.shape, 0)
    lane = iota(matrices.shape, 1)
    keep = ((row & 1) == (lane & 1)) & (((row >> 5) & 1) == (lane >> 6))
    matrices = jnp.where(keep, matrices, 0.0)
    for i in range(pairs):
        north = matrices[i * 64:i * 64 + 32]
        south = matrices[i * 64 + 32:i * 64 + 64]
        fold = jnp.concatenate([north + south, north - south], 0).astype(bf16)
        values = jnp.concatenate(
            [own[i, 0:32], other[i, 0:32], own[i, 32:64], other[i, 32:64]], 0
        )
        mixed = jnp.dot(fold, values, preferred_element_type=f32)
        stacked = jnp.concatenate(
            [mixed[0:32, :128], mixed[0:32, 128:], mixed[32:64, :128], mixed[32:64, 128:]], 0
        )
        turned = stacked.T
        pair = step * pairs + i
        rows_out[pl.ds(2 * pair, 64, stride=40), :] = turned[0:64]
        rows_out[pl.ds(2 * pair + 1, 64, stride=40), :] = turned[64:128]

    @pl.when(step == pl.num_programs(0) - 1)
    def _():
        out[...] = rows_out[...].astype(bf16)


def mix(inverses, own, other):
    pair_total = own.shape[0]
    step = MIX_PAIRS
    return pl.pallas_call(
        mix_kernel,
        out_shape=jax.ShapeDtypeStruct((2560, 128), bf16),
        grid=(pair_total // step,),
        in_specs=[
            pl.BlockSpec((step * 64, 32), lambda i: (i, 0)),
            pl.BlockSpec((step, 64, 256), lambda i: (i, 0, 0)),
            pl.BlockSpec((step, 64, 256), lambda i: (i, 0, 0)),
        ],
        out_specs=pl.BlockSpec((2560, 128), lambda i: (0, 0)),
        scratch_shapes=[pltpu.VMEM((2560, 128), f32)],
        compiler_params=pltpu.CompilerParams(vmem_limit_bytes=VMEM_LIMIT),
        name="mix",
    )(inverses, own, other)


def legendre_kernel(waves, own, other, table, out, even, odd, folded):
    slot = pl.program_id(0)
    parity = pl.program_id(1)
    slab = lax.axis_index("lev")
    owner = lax.axis_index("lat")
    degree_rows = table.shape[2]

    @pl.when((slot == 0) & (parity == 0))
    def _():
        row = iota((256, 256), 0)
        target = (
            ((row >> 6) & 1) * 128 + ((row >> 5) & 1) * 64 + ((row >> 7) ^ slab) * 32 + (row & 31)
        )
        order = (iota((256, 256), 1) == target).astype(f32).astype(bf16)
        both = jnp.concatenate([own[...], other[...]], 1)
        ordered = jnp.dot(both, order, preferred_element_type=f32)
        even[...] = ordered[:, :128]
        odd[...] = ordered[:, 128:]
        for s in range(2):
            folded[s, 0] = even[pl.ds(s, 1280, stride=2), :].astype(bf16)
            folded[s, 1] = odd[pl.ds(s, 1280, stride=2), :].astype(bf16)

    summed = jnp.dot(table[0, 0], folded[slot, parity], preferred_element_type=f32)
    wave = waves[owner * 2 + slot]
    degree = wave + 2 * (slab * degree_rows + iota(summed.shape, 0)) + parity
    out[0, 0] = jnp.where(degree <= TRUNC, summed, 0.0).astype(bf16)


def legendre_sum(wave_table, own, other, table):
    slots, parities, degree_rows, pairs = table.shape
    return pl.pallas_call(
        legendre_kernel,
        out_shape=jax.ShapeDtypeStruct((slots, parities, degree_rows, 128), bf16),
        grid=(slots, parities),
        in_specs=[
            pl.BlockSpec(memory_space=pltpu.SMEM),
            pl.BlockSpec((2560, 128), lambda s, q: (0, 0)),
            pl.BlockSpec((2560, 128), lambda s, q: (0, 0)),
            pl.BlockSpec((1, 1, degree_rows, pairs), lambda s, q: (s, q, 0, 0)),
        ],
        out_specs=pl.BlockSpec((1, 1, degree_rows, 128), lambda s, q: (s, q, 0, 0)),
        scratch_shapes=[
            pltpu.VMEM((2560, 128), f32),
            pltpu.VMEM((2560, 128), f32),
            pltpu.VMEM((2, 2, 1280, 128), bf16),
        ],
        compiler_params=pltpu.CompilerParams(vmem_limit_bytes=VMEM_LIMIT),
        name="legendre",
    )(wave_table, own, other, table)


def on_device(grid_values, lat_counts, wave_table, inverses, legendre):
    pair_total = lat_counts.shape[0]
    slab_width = grid_values.shape[1]
    grouped = grid_values.reshape(pair_total, 2 * slab_width, grid_values.shape[2])
    swap = [(0, 1), (1, 0)]
    own = fourier(grouped, lat_counts, wave_table)
    other = lax.ppermute(own, "lev", swap)
    half = lax.dynamic_slice_in_dim(inverses, lax.axis_index("lev") * 16, 16, 2)
    half = half.astype(bf16).transpose(0, 2, 1, 3).reshape(2 * pair_total * 32, 32)
    send = mix(half, own, other)
    slab = lax.all_to_all(
        send.reshape(64, 40, 128), "lat", split_axis=0, concat_axis=0, tiled=True
    )
    rest = lax.ppermute(slab, "lev", swap)
    return legendre_sum(wave_table, slab.reshape(2560, 128), rest.reshape(2560, 128), legendre)


def solution(mesh):
    placed = (
        P("lat", "lev", None),
        P("lat"),
        P(),
        P("lat", None, None, None),
        P("lat", None, "lev", None),
    )
    return jax.shard_map(
        on_device,
        mesh=mesh,
        in_specs=placed,
        out_specs=P("lat", None, "lev", None),
        check_vma=False,
    )
```

```python
import functools

import jax
import jax.numpy as jnp
from jax import lax
from jax.experimental import pallas as pl
from jax.experimental.pallas import tpu as pltpu
from jax.sharding import PartitionSpec as P

TRUNC = 1279
BLOCK = 256
GROUP = 4
AHEAD = 8
MIX_PAIRS = 5
FOURIER_VMEM = 53 * 2**20
MIX_VMEM = 48 * 2**20
LEGENDRE_VMEM = 24 * 2**20

COS_TERMS = (1.0, -19.73920440673828, 64.9391098022461, -85.45005798339844,
             60.16698455810547, -25.965150833129883, 6.525190353393555)
SIN_TERMS = (6.2831854820251465, -41.34170150756836, 81.60513305664062, -76.7029800415039,
             42.02566146850586, -14.898837089538574, 3.236703872680664)

f32 = jnp.float32
bf16 = jnp.bfloat16


def horner(z, terms):
    total = jnp.full_like(z, terms[-1])
    for term in terms[-2::-1]:
        total = total * z + term
    return total


def iota(shape, dim):
    return lax.broadcasted_iota(jnp.int32, shape, dim)


def fourier_kernel(numbers, waves, grid, out, values, bases, turns, tail, sems):
    pairs, rows, storage = grid.shape
    counts = numbers.at[pl.ds(128, pairs)]
    blocks = storage // BLOCK
    rest = storage - blocks * BLOCK

    def fetch(p):
        return pltpu.make_async_copy(grid.at[p], values.at[p], sems.at[p])

    for p in range(AHEAD):
        fetch(p).start()

    table = jnp.broadcast_to(waves[:, 0:128], (8, 128))
    order = iota((128, 128), 0) == (iota((128, 128), 1) % 64) * 2 + iota((128, 128), 1) // 64
    order = order.astype(f32).astype(bf16)
    high = jnp.dot((table // 64).astype(f32).astype(bf16), order, preferred_element_type=f32)
    low = jnp.dot((table % 64).astype(f32).astype(bf16), order, preferred_element_type=f32)
    wave_row = (high * 64.0 + low)[0:1]
    tail[...] = jnp.zeros_like(tail)
    row = iota((40, 128), 0)
    position = jnp.where(row < 16, row, jnp.where(row < 32, (row - 16) * 16, BLOCK)).astype(f32)
    angle_index = position * wave_row
    lane = iota((16, BLOCK), 1).astype(f32).astype(bf16)

    def make_basis(p):
        count_f = jnp.full((8, 128), counts[p], jnp.int32).astype(f32)
        inverse = 1.0 / count_f
        inverse5 = jnp.concatenate([inverse] * 5, 0)
        count5 = jnp.concatenate([count_f] * 5, 0)
        whole = jnp.floor(angle_index * inverse5 + 0.5)
        u = (angle_index - whole * count5) * inverse5
        z = u * u
        cosine = horner(z, COS_TERMS)
        sine = u * horner(z, SIN_TERMS)
        cos_fine, sin_fine = cosine[0:16], sine[0:16]
        for a in range(16):
            c, s = cosine[16 + a:17 + a], sine[16 + a:17 + a]
            bases[p, a * 16:(a + 1) * 16, 0:128] = (c * cos_fine - s * sin_fine).astype(bf16)
            bases[p, a * 16:(a + 1) * 16, 128:256] = (-(s * cos_fine + c * sin_fine)).astype(bf16)
        turns[p] = jnp.concatenate([cosine[32:40], -sine[32:40], inverse], 0)

    def clear_beyond(piece, first, count):
        limit = jnp.full((16, BLOCK), jnp.clip(count - first, 0, BLOCK), jnp.int32)
        inside = lane < limit.astype(f32).astype(bf16)
        zero = jnp.zeros((16, BLOCK), bf16)
        return jnp.concatenate(
            [jnp.where(inside, piece[r:r + 16], zero) for r in range(0, rows, 16)], 0
        )

    def transform(p, i):
        count = counts[p]
        tail[i, :, 0:rest] = values[p, :, blocks * BLOCK:storage]
        pieces = [clear_beyond(tail[i], blocks * BLOCK, count)]
        pieces += [values[p, :, b * BLOCK:(b + 1) * BLOCK] for b in range(blocks - 1, -1, -1)]
        product = jnp.dot(jnp.concatenate(pieces, 0), bases[p], preferred_element_type=f32)
        turn_r, turn_i, scale = turns[p, 0:1], turns[p, 8:9], turns[p, 16:17]
        real, imag = product[0:rows, :128], product[0:rows, 128:]
        for b in range(blocks - 1, -1, -1):
            used = jnp.where((b + 1) * BLOCK < count, 1.0, 0.0)
            step_r, step_i = turn_r * used, turn_i * used
            at = (blocks - b) * rows
            new_r, new_i = product[at:at + rows, :128], product[at:at + rows, 128:]
            real, imag = (
                real * step_r - imag * step_i + new_r,
                real * step_i + imag * step_r + new_i,
            )
        out[p] = jnp.concatenate([real * scale, imag * scale], 1).astype(bf16)

    def basis_step(t, carry):
        for i in range(GROUP):
            make_basis(t * GROUP + i)
        return carry

    lax.fori_loop(0, pairs // GROUP, basis_step, 0)

    def group_step(t, carry):
        @pl.when(t * GROUP + AHEAD < pairs)
        def _():
            for i in range(GROUP):
                fetch(t * GROUP + AHEAD + i).start()

        for i in range(GROUP):
            fetch(t * GROUP + i).wait()
        for i in range(GROUP):
            p = t * GROUP + i
            first = jnp.minimum(counts[p] // BLOCK, blocks - 1) * BLOCK
            at = pl.ds(pl.multiple_of(first, BLOCK), BLOCK)
            values[p, :, at] = clear_beyond(values[p, :, at], first, counts[p])
        for i in range(GROUP):
            transform(t * GROUP + i, i)
        return carry

    lax.fori_loop(0, pairs // GROUP, group_step, 0)


def fourier(grouped, lat_counts, wave_table):
    pairs, rows, storage = grouped.shape
    numbers = jnp.pad(jnp.concatenate([wave_table, lat_counts]), (0, 128 - pairs))
    return pl.pallas_call(
        fourier_kernel,
        out_shape=jax.ShapeDtypeStruct((pairs, rows, 256), bf16),
        in_specs=[
            pl.BlockSpec(memory_space=pltpu.SMEM),
            pl.BlockSpec(memory_space=pltpu.VMEM),
            pl.BlockSpec(memory_space=pl.ANY),
        ],
        out_specs=pl.BlockSpec(memory_space=pltpu.VMEM),
        scratch_shapes=[
            pltpu.VMEM((pairs, rows, storage), bf16),
            pltpu.VMEM((pairs, BLOCK, 256), bf16),
            pltpu.VMEM((pairs, 24, 128), f32),
            pltpu.VMEM((GROUP, rows, BLOCK), bf16),
            pltpu.SemaphoreType.DMA((pairs,)),
        ],
        compiler_params=pltpu.CompilerParams(vmem_limit_bytes=FOURIER_VMEM),
        name="fourier",
    )(numbers, numbers.reshape(1, 256), grouped)


def mix_kernel(inverses, own, other, table, out, table_out, rows_out, sem):
    bring = pltpu.make_async_copy(table, table_out, sem)
    bring.start()
    slab = lax.axis_index("lev")
    pairs = own.shape[0]
    lane = iota((32, 128), 1)
    level = (((lane >> 5) & 1) ^ slab) * 16 + ((lane >> 1) & 15)
    spread = (iota((32, 128), 0) == level).astype(f32).astype(bf16)
    row = iota((64 * MIX_PAIRS, 128), 0)
    lane = iota((64 * MIX_PAIRS, 128), 1)
    keep = ((row & 1) == (lane & 1)) & (((row >> 5) & 1) == (lane >> 6))

    def group_step(t, carry):
        first = pl.multiple_of(t * 64 * MIX_PAIRS, 64 * MIX_PAIRS)
        matrices = jnp.dot(
            inverses[pl.ds(first, 64 * MIX_PAIRS), :], spread, preferred_element_type=f32
        )
        matrices = jnp.where(keep, matrices, 0.0)
        for i in range(MIX_PAIRS):
            pair = t * MIX_PAIRS + i
            north = matrices[i * 64:i * 64 + 32]
            south = matrices[i * 64 + 32:i * 64 + 64]
            fold = jnp.concatenate([north + south, north - south], 0).astype(bf16)
            mine, theirs = own[pair], other[pair]
            values = jnp.concatenate([mine[0:32], theirs[0:32], mine[32:64], theirs[32:64]], 0)
            mixed = jnp.dot(fold, values, preferred_element_type=f32)
            stacked = jnp.concatenate(
                [mixed[0:32, :128], mixed[0:32, 128:], mixed[32:64, :128], mixed[32:64, 128:]], 0
            )
            turned = stacked.T
            rows_out[pl.ds(2 * pair, 64, stride=40), :] = turned[0:64]
            rows_out[pl.ds(2 * pair + 1, 64, stride=40), :] = turned[64:128]
        return carry

    lax.fori_loop(0, pairs // MIX_PAIRS, group_step, 0)
    out[...] = rows_out[...].astype(bf16)
    bring.wait()


def mix(inverses, own, other, table):
    return pl.pallas_call(
        mix_kernel,
        out_shape=[
            jax.ShapeDtypeStruct((2560, 128), bf16),
            jax.ShapeDtypeStruct(table.shape, table.dtype),
        ],
        in_specs=[pl.BlockSpec(memory_space=pltpu.VMEM)] * 3
        + [pl.BlockSpec(memory_space=pl.ANY)],
        out_specs=[pl.BlockSpec(memory_space=pltpu.VMEM)] * 2,
        scratch_shapes=[pltpu.VMEM((2560, 128), f32), pltpu.SemaphoreType.DMA],
        compiler_params=pltpu.CompilerParams(vmem_limit_bytes=MIX_VMEM),
        name="mix",
    )(inverses, own, other, table)


def legendre_kernel(waves, own, other, table, out, even, odd):
    slots, parities, degree_rows, pairs = table.shape
    slab = lax.axis_index("lev")
    owner = lax.axis_index("lat")
    row = iota((256, 256), 0)
    target = (
        ((row >> 6) & 1) * 128 + ((row >> 5) & 1) * 64 + ((row >> 7) ^ slab) * 32 + (row & 31)
    )
    order = (iota((256, 256), 1) == target).astype(f32).astype(bf16)
    both = jnp.concatenate([own[...], other[...]], 1)
    ordered = jnp.dot(both, order, preferred_element_type=f32)
    even[...] = ordered[:, :128]
    odd[...] = ordered[:, 128:]
    for s in range(slots):
        for q in range(parities):
            half = even if q == 0 else odd
            folded = half[pl.ds(s, pairs, stride=slots), :].astype(bf16)
            summed = jnp.dot(table[s, q], folded, preferred_element_type=f32)
            wave = waves[owner * slots + s]
            degree = wave + 2 * (slab * degree_rows + iota(summed.shape, 0)) + q
            out[s, q] = jnp.where(degree <= TRUNC, summed, 0.0).astype(bf16)


def legendre_sum(wave_table, own, other, table):
    slots, parities, degree_rows, pairs = table.shape
    return pl.pallas_call(
        legendre_kernel,
        out_shape=jax.ShapeDtypeStruct((slots, parities, degree_rows, 128), bf16),
        in_specs=[pl.BlockSpec(memory_space=pltpu.SMEM)]
        + [pl.BlockSpec(memory_space=pltpu.VMEM)] * 3,
        out_specs=pl.BlockSpec(memory_space=pltpu.VMEM),
        scratch_shapes=[pltpu.VMEM((slots * pairs, 128), f32)] * 2,
        compiler_params=pltpu.CompilerParams(vmem_limit_bytes=LEGENDRE_VMEM),
        name="legendre",
    )(wave_table, own, other, table)


def on_device(grid_values, lat_counts, wave_table, inverses, legendre):
    pair_total = lat_counts.shape[0]
    slab_width = grid_values.shape[1]
    grouped = grid_values.reshape(pair_total, 2 * slab_width, grid_values.shape[2])
    swap = [(0, 1), (1, 0)]
    own = fourier(grouped, lat_counts, wave_table)
    other = lax.ppermute(own, "lev", swap)
    half = lax.dynamic_slice_in_dim(inverses, lax.axis_index("lev") * 16, 16, 2)
    half = half.astype(bf16).transpose(0, 2, 1, 3).reshape(2 * pair_total * 32, 32)
    send, table = mix(half, own, other, legendre)
    slab = lax.all_to_all(
        send.reshape(64, 40, 128), "lat", split_axis=0, concat_axis=0, tiled=True
    )
    rest = lax.ppermute(slab, "lev", swap)
    return legendre_sum(wave_table, slab.reshape(2560, 128), rest.reshape(2560, 128), table)


def solution(mesh):
    placed = (
        P("lat", "lev", None),
        P("lat"),
        P(),
        P("lat", None, None, None),
        P("lat", None, "lev", None),
    )
    return jax.shard_map(
        on_device,
        mesh=mesh,
        in_specs=placed,
        out_specs=P("lat", None, "lev", None),
        check_vma=False,
    )
```

```python
import functools

import jax
import jax.numpy as jnp
from jax import lax
from jax.experimental import pallas as pl
from jax.experimental.pallas import tpu as pltpu
from jax.sharding import PartitionSpec as P

TRUNC = 1279
BLOCK = 256
GROUP = 4
AHEAD = 8
FOURIER_VMEM = 53 * 2**20
FOLD_VMEM = 50 * 2**20
PREPARE_VMEM = 48 * 2**20
LEGENDRE_VMEM = 24 * 2**20

COS_TERMS = (1.0, -19.73920440673828, 64.9391098022461, -85.45005798339844,
             60.16698455810547, -25.965150833129883, 6.525190353393555)
SIN_TERMS = (6.2831854820251465, -41.34170150756836, 81.60513305664062, -76.7029800415039,
             42.02566146850586, -14.898837089538574, 3.236703872680664)

f32 = jnp.float32
bf16 = jnp.bfloat16


def horner(z, terms):
    total = jnp.full_like(z, terms[-1])
    for term in terms[-2::-1]:
        total = total * z + term
    return total


def iota(shape, dim):
    return lax.broadcasted_iota(jnp.int32, shape, dim)


def fourier_kernel(numbers, waves, grid, out, values, bases, turns, tail, sems):
    pairs, rows, storage = grid.shape
    counts = numbers.at[pl.ds(128, pairs)]
    blocks = storage // BLOCK
    rest = storage - blocks * BLOCK

    def fetch(p):
        return pltpu.make_async_copy(grid.at[p], values.at[p], sems.at[p])

    for p in range(AHEAD):
        fetch(p).start()

    table = jnp.broadcast_to(waves[:, 0:128], (8, 128))
    order = iota((128, 128), 0) == (iota((128, 128), 1) % 64) * 2 + iota((128, 128), 1) // 64
    order = order.astype(f32).astype(bf16)
    high = jnp.dot((table // 64).astype(f32).astype(bf16), order, preferred_element_type=f32)
    low = jnp.dot((table % 64).astype(f32).astype(bf16), order, preferred_element_type=f32)
    wave_row = (high * 64.0 + low)[0:1]
    tail[...] = jnp.zeros_like(tail)
    row = iota((40, 128), 0)
    position = jnp.where(row < 16, row, jnp.where(row < 32, (row - 16) * 16, BLOCK)).astype(f32)
    angle_index = position * wave_row
    lane = iota((16, BLOCK), 1).astype(f32).astype(bf16)

    def make_basis(p):
        count_f = jnp.full((8, 128), counts[p], jnp.int32).astype(f32)
        inverse = 1.0 / count_f
        inverse5 = jnp.concatenate([inverse] * 5, 0)
        count5 = jnp.concatenate([count_f] * 5, 0)
        whole = jnp.floor(angle_index * inverse5 + 0.5)
        u = (angle_index - whole * count5) * inverse5
        z = u * u
        cosine = horner(z, COS_TERMS)
        sine = u * horner(z, SIN_TERMS)
        cos_fine, sin_fine = cosine[0:16], sine[0:16]
        for a in range(16):
            c, s = cosine[16 + a:17 + a], sine[16 + a:17 + a]
            bases[p, a * 16:(a + 1) * 16, 0:128] = (c * cos_fine - s * sin_fine).astype(bf16)
            bases[p, a * 16:(a + 1) * 16, 128:256] = (-(s * cos_fine + c * sin_fine)).astype(bf16)
        turns[p] = jnp.concatenate([cosine[32:40], -sine[32:40], inverse], 0)

    def clear_beyond(piece, first, count):
        limit = jnp.full((16, BLOCK), jnp.clip(count - first, 0, BLOCK), jnp.int32)
        inside = lane < limit.astype(f32).astype(bf16)
        zero = jnp.zeros((16, BLOCK), bf16)
        return jnp.concatenate(
            [jnp.where(inside, piece[r:r + 16], zero) for r in range(0, rows, 16)], 0
        )

    def transform(p, i):
        count = counts[p]
        tail[i, :, 0:rest] = values[p, :, blocks * BLOCK:storage]
        pieces = [clear_beyond(tail[i], blocks * BLOCK, count)]
        pieces += [values[p, :, b * BLOCK:(b + 1) * BLOCK] for b in range(blocks - 1, -1, -1)]
        product = jnp.dot(jnp.concatenate(pieces, 0), bases[p], preferred_element_type=f32)
        turn_r, turn_i, scale = turns[p, 0:1], turns[p, 8:9], turns[p, 16:17]
        real, imag = product[0:rows, :128], product[0:rows, 128:]
        for b in range(blocks - 1, -1, -1):
            used = jnp.where((b + 1) * BLOCK < count, 1.0, 0.0)
            step_r, step_i = turn_r * used, turn_i * used
            at = (blocks - b) * rows
            new_r, new_i = product[at:at + rows, :128], product[at:at + rows, 128:]
            real, imag = (
                real * step_r - imag * step_i + new_r,
                real * step_i + imag * step_r + new_i,
            )
        out[p] = jnp.concatenate([real * scale, imag * scale], 1).astype(bf16)

    def basis_step(t, carry):
        for i in range(GROUP):
            make_basis(t * GROUP + i)
        return carry

    lax.fori_loop(0, pairs // GROUP, basis_step, 0)

    def group_step(t, carry):
        @pl.when(t * GROUP + AHEAD < pairs)
        def _():
            for i in range(GROUP):
                fetch(t * GROUP + AHEAD + i).start()

        for i in range(GROUP):
            fetch(t * GROUP + i).wait()
        for i in range(GROUP):
            p = t * GROUP + i
            first = jnp.minimum(counts[p] // BLOCK, blocks - 1) * BLOCK
            at = pl.ds(pl.multiple_of(first, BLOCK), BLOCK)
            values[p, :, at] = clear_beyond(values[p, :, at], first, counts[p])
        for i in range(GROUP):
            transform(t * GROUP + i, i)
        return carry

    lax.fori_loop(0, pairs // GROUP, group_step, 0)


def fourier(grouped, lat_counts, wave_table):
    pairs, rows, storage = grouped.shape
    numbers = jnp.pad(jnp.concatenate([wave_table, lat_counts]), (0, 128 - pairs))
    return pl.pallas_call(
        fourier_kernel,
        out_shape=jax.ShapeDtypeStruct((pairs, rows, 256), bf16),
        in_specs=[
            pl.BlockSpec(memory_space=pltpu.SMEM),
            pl.BlockSpec(memory_space=pltpu.VMEM),
            pl.BlockSpec(memory_space=pl.ANY),
        ],
        out_specs=pl.BlockSpec(memory_space=pltpu.VMEM),
        scratch_shapes=[
            pltpu.VMEM((pairs, rows, storage), bf16),
            pltpu.VMEM((pairs, BLOCK, 256), bf16),
            pltpu.VMEM((pairs, 24, 128), f32),
            pltpu.VMEM((GROUP, rows, BLOCK), bf16),
            pltpu.SemaphoreType.DMA((pairs,)),
        ],
        compiler_params=pltpu.CompilerParams(vmem_limit_bytes=FOURIER_VMEM),
        name="fourier",
    )(numbers, numbers.reshape(1, 256), grouped)


def fold_kernel(inverses, table, out, table_out, sem):
    bring = pltpu.make_async_copy(table.at[0], table_out, sem)
    bring.start()
    slab = lax.axis_index("lev")
    lane = iota((32, 128), 1)
    level = (((lane >> 5) & 1) ^ slab) * 16 + ((lane >> 1) & 15)
    spread = (iota((32, 128), 0) == level).astype(f32).astype(bf16)
    matrices = jnp.dot(inverses[...], spread, preferred_element_type=f32)
    row = iota(matrices.shape, 0)
    lane = iota(matrices.shape, 1)
    keep = ((row & 1) == (lane & 1)) & (((row >> 5) & 1) == (lane >> 6))
    matrices = jnp.where(keep, matrices, 0.0)
    for pair in range(out.shape[0]):
        north = matrices[pair * 64:pair * 64 + 32]
        south = matrices[pair * 64 + 32:pair * 64 + 64]
        out[pair] = jnp.concatenate([north + south, north - south], 0).astype(bf16)
    bring.wait()


def fold_matrices(inverses, table):
    return pl.pallas_call(
        fold_kernel,
        out_shape=[
            jax.ShapeDtypeStruct((inverses.shape[0] // 64, 64, 128), bf16),
            jax.ShapeDtypeStruct(table.shape[1:], table.dtype),
        ],
        in_specs=[pl.BlockSpec(memory_space=pltpu.VMEM), pl.BlockSpec(memory_space=pl.ANY)],
        out_specs=[pl.BlockSpec(memory_space=pltpu.VMEM)] * 2,
        scratch_shapes=[pltpu.SemaphoreType.DMA],
        compiler_params=pltpu.CompilerParams(vmem_limit_bytes=FOLD_VMEM),
        cost_estimate=pl.CostEstimate(flops=2**24, bytes_accessed=2**22, transcendentals=0),
        name="fold",
    )(inverses, table)


def mix_kernel(matrices, own, other, out, rows_out):
    for pair in range(own.shape[0]):
        mine, theirs = own[pair], other[pair]
        values = jnp.concatenate([mine[0:32], theirs[0:32], mine[32:64], theirs[32:64]], 0)
        mixed = jnp.dot(matrices[pair], values, preferred_element_type=f32)
        stacked = jnp.concatenate(
            [mixed[0:32, :128], mixed[0:32, 128:], mixed[32:64, :128], mixed[32:64, 128:]], 0
        )
        turned = stacked.T
        rows_out[pl.ds(2 * pair, 64, stride=40), :] = turned[0:64]
        rows_out[pl.ds(2 * pair + 1, 64, stride=40), :] = turned[64:128]
    out[...] = rows_out[...].astype(bf16)


def mix(matrices, own, other):
    return pl.pallas_call(
        mix_kernel,
        out_shape=jax.ShapeDtypeStruct((2560, 128), bf16),
        in_specs=[pl.BlockSpec(memory_space=pltpu.VMEM)] * 3,
        out_specs=pl.BlockSpec(memory_space=pltpu.VMEM),
        scratch_shapes=[pltpu.VMEM((2560, 128), f32)],
        compiler_params=pltpu.CompilerParams(vmem_limit_bytes=LEGENDRE_VMEM),
        name="mix",
    )(matrices, own, other)


def unfold(values, side, even, odd):
    slab = lax.axis_index("lev") ^ side
    row = iota((128, 256), 0)
    target = (row >> 6) * 128 + ((row >> 5) & 1) * 64 + slab * 32 + (row & 31)
    order = (iota((128, 256), 1) == target).astype(f32).astype(bf16)
    ordered = jnp.dot(values, order, preferred_element_type=f32)
    even[...] = ordered[:, :128]
    odd[...] = ordered[:, 128:]


def prepare_kernel(own, table, out, table_out, even, odd, sem):
    bring = pltpu.make_async_copy(table.at[1], table_out, sem)
    bring.start()
    slots, parities, pairs, _ = out.shape
    unfold(own[...], 0, even, odd)
    for s in range(slots):
        out[s, 0] = even[pl.ds(s, pairs, stride=slots), :].astype(bf16)
        out[s, 1] = odd[pl.ds(s, pairs, stride=slots), :].astype(bf16)
    bring.wait()


def prepare(own, table):
    slots, parities, _, pairs = table.shape
    return pl.pallas_call(
        prepare_kernel,
        out_shape=[
            jax.ShapeDtypeStruct((slots, parities, pairs, 128), bf16),
            jax.ShapeDtypeStruct(table.shape[1:], table.dtype),
        ],
        in_specs=[pl.BlockSpec(memory_space=pltpu.VMEM), pl.BlockSpec(memory_space=pl.ANY)],
        out_specs=[pl.BlockSpec(memory_space=pltpu.VMEM)] * 2,
        scratch_shapes=[pltpu.VMEM((slots * pairs, 128), f32)] * 2 + [pltpu.SemaphoreType.DMA],
        compiler_params=pltpu.CompilerParams(vmem_limit_bytes=PREPARE_VMEM),
        cost_estimate=pl.CostEstimate(
            flops=4 * slots * pairs * 128 * 128, bytes_accessed=2**22, transcendentals=0
        ),
        name="prepare",
    )(own, table)


def legendre_kernel(waves, folded, other, first_table, second_table, out, even, odd):
    slots, parities, degree_rows, _ = out.shape
    pairs = folded.shape[2]
    slab = lax.axis_index("lev")
    owner = lax.axis_index("lat")
    unfold(other[...], 1, even, odd)
    for s in range(slots):
        mine = iota((1, 128), 1) == owner * slots + s
        wave = jnp.sum(jnp.where(mine, waves[...], 0), axis=1, keepdims=True)
        table = (first_table, second_table)[s]
        for q in range(parities):
            half = even if q == 0 else odd
            both = folded[s, q] + half[pl.ds(s, pairs, stride=slots), :].astype(bf16)
            summed = jnp.dot(table[q], both, preferred_element_type=f32)
            degree = wave + 2 * (slab * degree_rows + iota(summed.shape, 0)) + q
            out[s, q] = jnp.where(degree <= TRUNC, summed, 0.0).astype(bf16)


def legendre_sum(wave_table, folded, other, first_table, second_table):
    slots, parities, pairs, _ = folded.shape
    degree_rows = first_table.shape[1]
    return pl.pallas_call(
        legendre_kernel,
        out_shape=jax.ShapeDtypeStruct((slots, parities, degree_rows, 128), bf16),
        in_specs=[pl.BlockSpec(memory_space=pltpu.VMEM)] * 5,
        out_specs=pl.BlockSpec(memory_space=pltpu.VMEM),
        scratch_shapes=[pltpu.VMEM((slots * pairs, 128), f32)] * 2,
        compiler_params=pltpu.CompilerParams(vmem_limit_bytes=LEGENDRE_VMEM),
        name="legendre",
    )(wave_table.reshape(1, 128), folded, other, first_table, second_table)


def on_device(grid_values, lat_counts, wave_table, inverses, legendre):
    pair_total = lat_counts.shape[0]
    slab_width = grid_values.shape[1]
    grouped = grid_values.reshape(pair_total, 2 * slab_width, grid_values.shape[2])
    swap = [(0, 1), (1, 0)]
    own = fourier(grouped, lat_counts, wave_table)
    other = lax.ppermute(own, "lev", swap)
    half = lax.dynamic_slice_in_dim(inverses, lax.axis_index("lev") * 16, 16, 2)
    half = half.astype(bf16).transpose(0, 2, 1, 3).reshape(2 * pair_total * 32, 32)
    matrices, first_table = fold_matrices(half, legendre)
    send = mix(matrices, own, other)
    slab = lax.all_to_all(
        send.reshape(64, 40, 128), "lat", split_axis=0, concat_axis=0, tiled=True
    )
    rest = lax.ppermute(slab, "lev", swap)
    folded, second_table = prepare(slab.reshape(2560, 128), legendre)
    return legendre_sum(
        wave_table, folded, rest.reshape(2560, 128), first_table, second_table
    )


def solution(mesh):
    placed = (
        P("lat", "lev", None),
        P("lat"),
        P(),
        P("lat", None, None, None),
        P("lat", None, "lev", None),
    )
    return jax.shard_map(
        on_device,
        mesh=mesh,
        in_specs=placed,
        out_specs=P("lat", None, "lev", None),
        check_vma=False,
    )
```

```python
import functools

import jax
import jax.numpy as jnp
from jax import lax
from jax.experimental import pallas as pl
from jax.experimental.pallas import tpu as pltpu
from jax.sharding import PartitionSpec as P

TRUNC = 1279
BLOCK = 256
GROUP = 4
AHEAD = 8
FOURIER_VMEM = 53 * 2**20
FOLD_VMEM = 51 * 2**20
PREPARE_VMEM = 48 * 2**20
LEGENDRE_VMEM = 24 * 2**20

COS_TERMS = (1.0, -19.73920440673828, 64.9391098022461, -85.45005798339844,
             60.16698455810547, -25.965150833129883, 6.525190353393555)
SIN_TERMS = (6.2831854820251465, -41.34170150756836, 81.60513305664062, -76.7029800415039,
             42.02566146850586, -14.898837089538574, 3.236703872680664)

f32 = jnp.float32
bf16 = jnp.bfloat16


def horner(z, terms):
    total = jnp.full_like(z, terms[-1])
    for term in terms[-2::-1]:
        total = total * z + term
    return total


def iota(shape, dim):
    return lax.broadcasted_iota(jnp.int32, shape, dim)


def fourier_kernel(numbers, waves, grid, out, values, bases, turns, tail, scalars, sems, scalar_sem):
    pairs, rows, storage = grid.shape
    counts = scalars.at[pl.ds(128, pairs)]
    blocks = storage // BLOCK
    rest = storage - blocks * BLOCK

    def fetch(p):
        return pltpu.make_async_copy(grid.at[p], values.at[p], sems.at[p])

    for p in range(AHEAD):
        fetch(p).start()
    bring = pltpu.make_async_copy(numbers, scalars, scalar_sem)
    bring.start()

    table = jnp.broadcast_to(waves[:, 0:128], (8, 128))
    order = iota((128, 128), 0) == (iota((128, 128), 1) % 64) * 2 + iota((128, 128), 1) // 64
    order = order.astype(f32).astype(bf16)
    high = jnp.dot((table // 64).astype(f32).astype(bf16), order, preferred_element_type=f32)
    low = jnp.dot((table % 64).astype(f32).astype(bf16), order, preferred_element_type=f32)
    wave_row = (high * 64.0 + low)[0:1]
    tail[...] = jnp.zeros_like(tail)
    row = iota((40, 128), 0)
    position = jnp.where(row < 16, row, jnp.where(row < 32, (row - 16) * 16, BLOCK)).astype(f32)
    angle_index = position * wave_row
    lane = iota((16, BLOCK), 1).astype(f32).astype(bf16)
    bring.wait()

    def make_basis(p):
        count_f = jnp.full((8, 128), counts[p], jnp.int32).astype(f32)
        inverse = 1.0 / count_f
        inverse5 = jnp.concatenate([inverse] * 5, 0)
        count5 = jnp.concatenate([count_f] * 5, 0)
        whole = jnp.floor(angle_index * inverse5 + 0.5)
        u = (angle_index - whole * count5) * inverse5
        z = u * u
        cosine = horner(z, COS_TERMS)
        sine = u * horner(z, SIN_TERMS)
        cos_fine, sin_fine = cosine[0:16], sine[0:16]
        for a in range(16):
            c, s = cosine[16 + a:17 + a], sine[16 + a:17 + a]
            bases[p, a * 16:(a + 1) * 16, 0:128] = (c * cos_fine - s * sin_fine).astype(bf16)
            bases[p, a * 16:(a + 1) * 16, 128:256] = (-(s * cos_fine + c * sin_fine)).astype(bf16)
        turns[p] = jnp.concatenate([cosine[32:40], -sine[32:40], inverse], 0)

    def clear_beyond(piece, first, count):
        limit = jnp.full((16, BLOCK), jnp.clip(count - first, 0, BLOCK), jnp.int32)
        inside = lane < limit.astype(f32).astype(bf16)
        zero = jnp.zeros((16, BLOCK), bf16)
        return jnp.concatenate(
            [jnp.where(inside, piece[r:r + 16], zero) for r in range(0, rows, 16)], 0
        )

    def transform(p, i):
        count = counts[p]
        tail[i, :, 0:rest] = values[p, :, blocks * BLOCK:storage]
        pieces = [clear_beyond(tail[i], blocks * BLOCK, count)]
        pieces += [values[p, :, b * BLOCK:(b + 1) * BLOCK] for b in range(blocks - 1, -1, -1)]
        product = jnp.dot(jnp.concatenate(pieces, 0), bases[p], preferred_element_type=f32)
        turn_r, turn_i, scale = turns[p, 0:1], turns[p, 8:9], turns[p, 16:17]
        real, imag = product[0:rows, :128], product[0:rows, 128:]
        for b in range(blocks - 1, -1, -1):
            used = jnp.where((b + 1) * BLOCK < count, 1.0, 0.0)
            step_r, step_i = turn_r * used, turn_i * used
            at = (blocks - b) * rows
            new_r, new_i = product[at:at + rows, :128], product[at:at + rows, 128:]
            real, imag = (
                real * step_r - imag * step_i + new_r,
                real * step_i + imag * step_r + new_i,
            )
        out[p] = jnp.concatenate([real * scale, imag * scale], 1).astype(bf16)

    def basis_step(t, carry):
        for i in range(GROUP):
            make_basis(t * GROUP + i)
        return carry

    lax.fori_loop(0, pairs // GROUP, basis_step, 0)

    def group_step(t, carry):
        @pl.when(t * GROUP + AHEAD < pairs)
        def _():
            for i in range(GROUP):
                fetch(t * GROUP + AHEAD + i).start()

        for i in range(GROUP):
            fetch(t * GROUP + i).wait()
        for i in range(GROUP):
            p = t * GROUP + i
            first = jnp.minimum(counts[p] // BLOCK, blocks - 1) * BLOCK
            at = pl.ds(pl.multiple_of(first, BLOCK), BLOCK)
            values[p, :, at] = clear_beyond(values[p, :, at], first, counts[p])
        for i in range(GROUP):
            transform(t * GROUP + i, i)
        return carry

    lax.fori_loop(0, pairs // GROUP, group_step, 0)


def fourier(grouped, lat_counts, wave_table):
    pairs, rows, storage = grouped.shape
    numbers = jnp.pad(jnp.concatenate([wave_table, lat_counts]), (0, 128 - pairs))
    return pl.pallas_call(
        fourier_kernel,
        out_shape=jax.ShapeDtypeStruct((pairs, rows, 256), bf16),
        in_specs=[
            pl.BlockSpec(memory_space=pl.ANY),
            pl.BlockSpec(memory_space=pltpu.VMEM),
            pl.BlockSpec(memory_space=pl.ANY),
        ],
        out_specs=pl.BlockSpec(memory_space=pltpu.VMEM),
        scratch_shapes=[
            pltpu.VMEM((pairs, rows, storage), bf16),
            pltpu.VMEM((pairs, BLOCK, 256), bf16),
            pltpu.VMEM((pairs, 24, 128), f32),
            pltpu.VMEM((GROUP, rows, BLOCK), bf16),
            pltpu.SMEM((256,), jnp.int32),
            pltpu.SemaphoreType.DMA((pairs,)),
            pltpu.SemaphoreType.DMA,
        ],
        compiler_params=pltpu.CompilerParams(vmem_limit_bytes=FOURIER_VMEM),
        name="fourier",
    )(numbers, numbers.reshape(1, 256), grouped)


def fold_kernel(inverses, table, out, table_out, sem):
    bring = pltpu.make_async_copy(table.at[0, 0], table_out, sem)
    bring.start()
    slab = lax.axis_index("lev")
    lane = iota((32, 128), 1)
    level = (((lane >> 5) & 1) ^ slab) * 16 + ((lane >> 1) & 15)
    spread = (iota((32, 128), 0) == level).astype(f32).astype(bf16)
    matrices = jnp.dot(inverses[...], spread, preferred_element_type=f32)
    row = iota(matrices.shape, 0)
    lane = iota(matrices.shape, 1)
    keep = ((row & 1) == (lane & 1)) & (((row >> 5) & 1) == (lane >> 6))
    matrices = jnp.where(keep, matrices, 0.0)
    for pair in range(out.shape[0]):
        north = matrices[pair * 64:pair * 64 + 32]
        south = matrices[pair * 64 + 32:pair * 64 + 64]
        out[pair] = jnp.concatenate([north + south, north - south], 0).astype(bf16)
    bring.wait()


def fold_matrices(inverses, table):
    return pl.pallas_call(
        fold_kernel,
        out_shape=[
            jax.ShapeDtypeStruct((inverses.shape[0] // 64, 64, 128), bf16),
            jax.ShapeDtypeStruct(table.shape[2:], table.dtype),
        ],
        in_specs=[pl.BlockSpec(memory_space=pltpu.VMEM), pl.BlockSpec(memory_space=pl.ANY)],
        out_specs=[pl.BlockSpec(memory_space=pltpu.VMEM)] * 2,
        scratch_shapes=[pltpu.SemaphoreType.DMA],
        compiler_params=pltpu.CompilerParams(vmem_limit_bytes=FOLD_VMEM),
        cost_estimate=pl.CostEstimate(flops=2**24, bytes_accessed=2**22, transcendentals=0),
        name="fold",
    )(inverses, table)


def mix_kernel(matrices, own, other, out, rows_out):
    for pair in range(own.shape[0]):
        mine, theirs = own[pair], other[pair]
        values = jnp.concatenate([mine[0:32], theirs[0:32], mine[32:64], theirs[32:64]], 0)
        mixed = jnp.dot(matrices[pair], values, preferred_element_type=f32)
        stacked = jnp.concatenate(
            [mixed[0:32, :128], mixed[32:64, :128], mixed[0:32, 128:], mixed[32:64, 128:]], 0
        )
        turned = stacked.T
        rows_out[pl.ds(2 * pair, 64, stride=40), :] = turned[0:64]
        rows_out[pl.ds(2 * pair + 1, 64, stride=40), :] = turned[64:128]
    out[...] = rows_out[...].astype(bf16)


def mix(matrices, own, other):
    return pl.pallas_call(
        mix_kernel,
        out_shape=jax.ShapeDtypeStruct((2560, 128), bf16),
        in_specs=[pl.BlockSpec(memory_space=pltpu.VMEM)] * 3,
        out_specs=pl.BlockSpec(memory_space=pltpu.VMEM),
        scratch_shapes=[pltpu.VMEM((2560, 128), f32)],
        compiler_params=pltpu.CompilerParams(vmem_limit_bytes=LEGENDRE_VMEM),
        name="mix",
    )(matrices, own, other)


def unfold(rows, slab):
    return rows, pltpu.roll(rows, jnp.where(slab == 0, 96, 32), 1)


def prepare_kernel(own, table, out, table_out, rows, sems):
    bring = [
        pltpu.make_async_copy(table.at[0, 1], table_out.at[0], sems.at[0]),
        pltpu.make_async_copy(table.at[1], table_out.at[pl.ds(1, 2)], sems.at[1]),
    ]
    for copy in bring:
        copy.start()
    slots, parities, pairs, _ = out.shape
    slab = lax.axis_index("lev")
    rows[...] = own[...].astype(f32)
    for s in range(slots):
        same, opposite = unfold(rows[pl.ds(s, pairs, stride=slots), :], slab)
        out[s, slab] = same.astype(bf16)
        out[s, 1 - slab] = opposite.astype(bf16)
    for copy in bring:
        copy.wait()


def prepare(own, table):
    slots, parities, _, pairs = table.shape
    return pl.pallas_call(
        prepare_kernel,
        out_shape=[
            jax.ShapeDtypeStruct((slots, parities, pairs, 128), bf16),
            jax.ShapeDtypeStruct((3,) + table.shape[2:], table.dtype),
        ],
        in_specs=[pl.BlockSpec(memory_space=pltpu.VMEM), pl.BlockSpec(memory_space=pl.ANY)],
        out_specs=[pl.BlockSpec(memory_space=pltpu.VMEM)] * 2,
        scratch_shapes=[pltpu.VMEM((slots * pairs, 128), f32)] + [
            pltpu.SemaphoreType.DMA((2,))
        ],
        compiler_params=pltpu.CompilerParams(vmem_limit_bytes=PREPARE_VMEM),
        cost_estimate=pl.CostEstimate(
            flops=4 * slots * pairs * 128 * 128, bytes_accessed=2**22, transcendentals=0
        ),
        name="prepare",
    )(own, table)


def legendre_kernel(waves, folded, other, first_table, second_table, out, rows, both):
    slots, parities, degree_rows, _ = out.shape
    pairs = folded.shape[2]
    slab = lax.axis_index("lev")
    owner = lax.axis_index("lat")
    rows[...] = other[...].astype(f32)
    mine = (((iota((16, 128), 1) >> 5) & 1) == slab).astype(f32).astype(bf16) > 0
    mine = jnp.broadcast_to(mine[0:1], (pairs, 128))
    for s in range(slots):
        same, opposite = unfold(rows[pl.ds(s, pairs, stride=slots), :], 1 - slab)
        both[s, 1 - slab] = jnp.where(mine, folded[s, 1 - slab], same.astype(bf16))
        both[s, slab] = jnp.where(mine, folded[s, slab], opposite.astype(bf16))
    for s in range(slots):
        here = iota((1, 128), 1) == owner * slots + s
        wave = jnp.sum(jnp.where(here, waves[...], 0), axis=1, keepdims=True)
        for q in range(parities):
            table = first_table[...] if s + q == 0 else second_table[s * parities + q - 1]
            summed = jnp.dot(table, both[s, q], preferred_element_type=f32)
            degree = wave + 2 * (slab * degree_rows + iota(summed.shape, 0)) + q
            out[s, q] = jnp.where(degree <= TRUNC, summed, 0.0).astype(bf16)


def legendre_sum(wave_table, folded, other, first_table, second_table):
    slots, parities, pairs, _ = folded.shape
    degree_rows = first_table.shape[0]
    return pl.pallas_call(
        legendre_kernel,
        out_shape=jax.ShapeDtypeStruct((slots, parities, degree_rows, 128), bf16),
        in_specs=[pl.BlockSpec(memory_space=pltpu.VMEM)] * 5,
        out_specs=pl.BlockSpec(memory_space=pltpu.VMEM),
        scratch_shapes=[
            pltpu.VMEM((slots * pairs, 128), f32),
            pltpu.VMEM((slots, parities, pairs, 128), bf16),
        ],
        compiler_params=pltpu.CompilerParams(vmem_limit_bytes=LEGENDRE_VMEM),
        name="legendre",
    )(wave_table.reshape(1, 128), folded, other, first_table, second_table)


def on_device(grid_values, lat_counts, wave_table, inverses, legendre):
    pair_total = lat_counts.shape[0]
    slab_width = grid_values.shape[1]
    grouped = grid_values.reshape(pair_total, 2 * slab_width, grid_values.shape[2])
    swap = [(0, 1), (1, 0)]
    own = fourier(grouped, lat_counts, wave_table)
    other = lax.ppermute(own, "lev", swap)
    half = lax.dynamic_slice_in_dim(inverses, lax.axis_index("lev") * 16, 16, 2)
    half = half.astype(bf16).transpose(0, 2, 1, 3).reshape(2 * pair_total * 32, 32)
    matrices, first_table = fold_matrices(half, legendre)
    send = mix(matrices, own, other)
    slab = lax.all_to_all(
        send.reshape(64, 40, 128), "lat", split_axis=0, concat_axis=0, tiled=True
    )
    rest = lax.ppermute(slab, "lev", swap)
    folded, second_table = prepare(slab.reshape(2560, 128), legendre)
    return legendre_sum(
        wave_table, folded, rest.reshape(2560, 128), first_table, second_table
    )


def solution(mesh):
    placed = (
        P("lat", "lev", None),
        P("lat"),
        P(),
        P("lat", None, None, None),
        P("lat", None, "lev", None),
    )
    return jax.shard_map(
        on_device,
        mesh=mesh,
        in_specs=placed,
        out_specs=P("lat", None, "lev", None),
        check_vma=False,
    )
```

```python
import functools

import jax
import jax.numpy as jnp
from jax import lax
from jax.experimental import pallas as pl
from jax.experimental.pallas import tpu as pltpu
from jax.sharding import PartitionSpec as P

TRUNC = 1279
BLOCK = 256
GROUPS = (4, 4, 4, 4, 2, 2)
AHEAD = 16
FOURIER_VMEM = 53 * 2**20
FOLD_VMEM = 51 * 2**20
PREPARE_VMEM = 48 * 2**20
LEGENDRE_VMEM = 24 * 2**20

COS_TERMS = (1.0, -19.73920440673828, 64.9391098022461, -85.45005798339844,
             60.16698455810547, -25.965150833129883, 6.525190353393555)
SIN_TERMS = (6.2831854820251465, -41.34170150756836, 81.60513305664062, -76.7029800415039,
             42.02566146850586, -14.898837089538574, 3.236703872680664)

f32 = jnp.float32
bf16 = jnp.bfloat16


def horner(z, terms):
    total = jnp.full_like(z, terms[-1])
    for term in terms[-2::-1]:
        total = total * z + term
    return total


def iota(shape, dim):
    return lax.broadcasted_iota(jnp.int32, shape, dim)


def fourier_kernel(numbers, waves, grid, out, values, bases, turns, tail, scalars, sems, scalar_sem):
    pairs, rows, storage = grid.shape
    counts = scalars.at[pl.ds(128, pairs)]
    blocks = storage // BLOCK
    rest = storage - blocks * BLOCK

    def fetch(p):
        return pltpu.make_async_copy(grid.at[p], values.at[p], sems.at[p])

    for p in range(AHEAD):
        fetch(p).start()
    bring = pltpu.make_async_copy(numbers, scalars, scalar_sem)
    bring.start()

    table = jnp.broadcast_to(waves[:, 0:128], (8, 128))
    order = iota((128, 128), 0) == (iota((128, 128), 1) % 64) * 2 + iota((128, 128), 1) // 64
    order = order.astype(f32).astype(bf16)
    high = jnp.dot((table // 64).astype(f32).astype(bf16), order, preferred_element_type=f32)
    low = jnp.dot((table % 64).astype(f32).astype(bf16), order, preferred_element_type=f32)
    wave_row = (high * 64.0 + low)[0:1]
    tail[...] = jnp.zeros_like(tail)
    row = iota((40, 128), 0)
    position = jnp.where(row < 16, row, jnp.where(row < 32, (row - 16) * 16, BLOCK)).astype(f32)
    angle_index = position * wave_row
    lane = iota((16, BLOCK), 1).astype(f32).astype(bf16)
    bring.wait()

    def make_basis(p):
        count_f = jnp.full((8, 128), counts[p], jnp.int32).astype(f32)
        inverse = 1.0 / count_f
        inverse5 = jnp.concatenate([inverse] * 5, 0)
        count5 = jnp.concatenate([count_f] * 5, 0)
        whole = jnp.floor(angle_index * inverse5 + 0.5)
        u = (angle_index - whole * count5) * inverse5
        z = u * u
        cosine = horner(z, COS_TERMS)
        sine = u * horner(z, SIN_TERMS)
        cos_fine, sin_fine = cosine[0:16], sine[0:16]
        for a in range(16):
            c, s = cosine[16 + a:17 + a], sine[16 + a:17 + a]
            bases[p, a * 16:(a + 1) * 16, 0:128] = (c * cos_fine - s * sin_fine).astype(bf16)
            bases[p, a * 16:(a + 1) * 16, 128:256] = (-(s * cos_fine + c * sin_fine)).astype(bf16)
        turns[p] = jnp.concatenate([cosine[32:40], -sine[32:40], inverse], 0)

    def clear_beyond(piece, first, count):
        limit = jnp.full((16, BLOCK), jnp.clip(count - first, 0, BLOCK), jnp.int32)
        inside = lane < limit.astype(f32).astype(bf16)
        zero = jnp.zeros((16, BLOCK), bf16)
        return jnp.concatenate(
            [jnp.where(inside, piece[r:r + 16], zero) for r in range(0, rows, 16)], 0
        )

    def transform(p, i):
        count = counts[p]
        tail[i, :, 0:rest] = values[p, :, blocks * BLOCK:storage]
        pieces = [clear_beyond(tail[i], blocks * BLOCK, count)]
        pieces += [values[p, :, b * BLOCK:(b + 1) * BLOCK] for b in range(blocks - 1, -1, -1)]
        product = jnp.dot(jnp.concatenate(pieces, 0), bases[p], preferred_element_type=f32)
        turn_r, turn_i, scale = turns[p, 0:1], turns[p, 8:9], turns[p, 16:17]
        real, imag = product[0:rows, :128], product[0:rows, 128:]
        for b in range(blocks - 1, -1, -1):
            used = jnp.where((b + 1) * BLOCK < count, 1.0, 0.0)
            step_r, step_i = turn_r * used, turn_i * used
            at = (blocks - b) * rows
            new_r, new_i = product[at:at + rows, :128], product[at:at + rows, 128:]
            real, imag = (
                real * step_r - imag * step_i + new_r,
                real * step_i + imag * step_r + new_i,
            )
        out[p] = jnp.concatenate([real * scale, imag * scale], 1).astype(bf16)

    starts = [sum(GROUPS[:g]) for g in range(len(GROUPS))]
    for p in range(pairs):
        make_basis(p)
    fetched = AHEAD
    for begin, size in zip(starts, GROUPS):
        group = range(begin, begin + size)
        for p in range(fetched, min(pairs, begin + AHEAD + size)):
            fetch(p).start()
            fetched = p + 1
        for p in group:
            fetch(p).wait()
        for p in group:
            first = jnp.minimum(counts[p] // BLOCK, blocks - 1) * BLOCK
            at = pl.ds(pl.multiple_of(first, BLOCK), BLOCK)
            values[p, :, at] = clear_beyond(values[p, :, at], first, counts[p])
        for p in group:
            transform(p, p - begin)


def fourier(grouped, lat_counts, wave_table):
    pairs, rows, storage = grouped.shape
    numbers = jnp.pad(jnp.concatenate([wave_table, lat_counts]), (0, 128 - pairs))
    return pl.pallas_call(
        fourier_kernel,
        out_shape=jax.ShapeDtypeStruct((pairs, rows, 256), bf16),
        in_specs=[
            pl.BlockSpec(memory_space=pl.ANY),
            pl.BlockSpec(memory_space=pltpu.VMEM),
            pl.BlockSpec(memory_space=pl.ANY),
        ],
        out_specs=pl.BlockSpec(memory_space=pltpu.VMEM),
        scratch_shapes=[
            pltpu.VMEM((pairs, rows, storage), bf16),
            pltpu.VMEM((pairs, BLOCK, 256), bf16),
            pltpu.VMEM((pairs, 24, 128), f32),
            pltpu.VMEM((max(GROUPS), rows, BLOCK), bf16),
            pltpu.SMEM((256,), jnp.int32),
            pltpu.SemaphoreType.DMA((pairs,)),
            pltpu.SemaphoreType.DMA,
        ],
        compiler_params=pltpu.CompilerParams(vmem_limit_bytes=FOURIER_VMEM),
        name="fourier",
    )(numbers, numbers.reshape(1, 256), grouped)


def fold_kernel(inverses, table, out, table_out, sem):
    bring = pltpu.make_async_copy(table.at[0, 0], table_out, sem)
    bring.start()
    slab = lax.axis_index("lev")
    lane = iota((32, 128), 1)
    level = (((lane >> 5) & 1) ^ slab) * 16 + ((lane >> 1) & 15)
    spread = (iota((32, 128), 0) == level).astype(f32).astype(bf16)
    matrices = jnp.dot(inverses[...], spread, preferred_element_type=f32)
    row = iota(matrices.shape, 0)
    lane = iota(matrices.shape, 1)
    keep = ((row & 1) == (lane & 1)) & (((row >> 5) & 1) == (lane >> 6))
    matrices = jnp.where(keep, matrices, 0.0)
    for pair in range(out.shape[0]):
        north = matrices[pair * 64:pair * 64 + 32]
        south = matrices[pair * 64 + 32:pair * 64 + 64]
        out[pair] = jnp.concatenate([north + south, north - south], 0).astype(bf16)
    bring.wait()


def fold_matrices(inverses, table):
    return pl.pallas_call(
        fold_kernel,
        out_shape=[
            jax.ShapeDtypeStruct((inverses.shape[0] // 64, 64, 128), bf16),
            jax.ShapeDtypeStruct(table.shape[2:], table.dtype),
        ],
        in_specs=[pl.BlockSpec(memory_space=pltpu.VMEM), pl.BlockSpec(memory_space=pl.ANY)],
        out_specs=[pl.BlockSpec(memory_space=pltpu.VMEM)] * 2,
        scratch_shapes=[pltpu.SemaphoreType.DMA],
        compiler_params=pltpu.CompilerParams(vmem_limit_bytes=FOLD_VMEM),
        cost_estimate=pl.CostEstimate(flops=2**24, bytes_accessed=2**22, transcendentals=0),
        name="fold",
    )(inverses, table)


def mix_kernel(matrices, own, other, out, rows_out):
    for pair in range(own.shape[0]):
        mine, theirs = own[pair], other[pair]
        values = jnp.concatenate([mine[0:32], theirs[0:32], mine[32:64], theirs[32:64]], 0)
        mixed = jnp.dot(matrices[pair], values, preferred_element_type=f32)
        stacked = jnp.concatenate(
            [mixed[0:32, :128], mixed[32:64, :128], mixed[0:32, 128:], mixed[32:64, 128:]], 0
        )
        turned = stacked.T
        rows_out[pl.ds(2 * pair, 64, stride=40), :] = turned[0:64]
        rows_out[pl.ds(2 * pair + 1, 64, stride=40), :] = turned[64:128]
    out[...] = rows_out[...].astype(bf16)


def mix(matrices, own, other):
    return pl.pallas_call(
        mix_kernel,
        out_shape=jax.ShapeDtypeStruct((2560, 128), bf16),
        in_specs=[pl.BlockSpec(memory_space=pltpu.VMEM)] * 3,
        out_specs=pl.BlockSpec(memory_space=pltpu.VMEM),
        scratch_shapes=[pltpu.VMEM((2560, 128), f32)],
        compiler_params=pltpu.CompilerParams(vmem_limit_bytes=LEGENDRE_VMEM),
        name="mix",
    )(matrices, own, other)


def unfold(rows, slab):
    return rows, pltpu.roll(rows, jnp.where(slab == 0, 96, 32), 1)


def prepare_kernel(own, table, out, table_out, rows, sems):
    bring = [
        pltpu.make_async_copy(table.at[0, 1], table_out.at[0], sems.at[0]),
        pltpu.make_async_copy(table.at[1], table_out.at[pl.ds(1, 2)], sems.at[1]),
    ]
    for copy in bring:
        copy.start()
    slots, parities, pairs, _ = out.shape
    slab = lax.axis_index("lev")
    rows[...] = own[...].astype(f32)
    for s in range(slots):
        same, opposite = unfold(rows[pl.ds(s, pairs, stride=slots), :], slab)
        out[s, slab] = same.astype(bf16)
        out[s, 1 - slab] = opposite.astype(bf16)
    for copy in bring:
        copy.wait()


def prepare(own, table):
    slots, parities, _, pairs = table.shape
    return pl.pallas_call(
        prepare_kernel,
        out_shape=[
            jax.ShapeDtypeStruct((slots, parities, pairs, 128), bf16),
            jax.ShapeDtypeStruct((3,) + table.shape[2:], table.dtype),
        ],
        in_specs=[pl.BlockSpec(memory_space=pltpu.VMEM), pl.BlockSpec(memory_space=pl.ANY)],
        out_specs=[pl.BlockSpec(memory_space=pltpu.VMEM)] * 2,
        scratch_shapes=[pltpu.VMEM((slots * pairs, 128), f32)] + [
            pltpu.SemaphoreType.DMA((2,))
        ],
        compiler_params=pltpu.CompilerParams(vmem_limit_bytes=PREPARE_VMEM),
        cost_estimate=pl.CostEstimate(
            flops=4 * slots * pairs * 128 * 128, bytes_accessed=2**22, transcendentals=0
        ),
        name="prepare",
    )(own, table)


def legendre_kernel(waves, folded, other, first_table, second_table, out, rows, both, done, sems):
    slots, parities, degree_rows, _ = out.shape
    pairs = folded.shape[2]
    slab = lax.axis_index("lev")
    owner = lax.axis_index("lat")
    rows[...] = other[...].astype(f32)
    mine = (((iota((16, 128), 1) >> 5) & 1) == slab).astype(f32).astype(bf16) > 0
    mine = jnp.broadcast_to(mine[0:1], (pairs, 128))
    for s in range(slots):
        same, opposite = unfold(rows[pl.ds(s, pairs, stride=slots), :], 1 - slab)
        both[s, 1 - slab] = jnp.where(mine, folded[s, 1 - slab], same.astype(bf16))
        both[s, slab] = jnp.where(mine, folded[s, slab], opposite.astype(bf16))
    stores = []
    for s in range(slots):
        here = iota((1, 128), 1) == owner * slots + s
        wave = jnp.sum(jnp.where(here, waves[...], 0), axis=1, keepdims=True)
        for q in range(parities):
            table = first_table[...] if s + q == 0 else second_table[s * parities + q - 1]
            summed = jnp.dot(table, both[s, q], preferred_element_type=f32)
            degree = wave + 2 * (slab * degree_rows + iota(summed.shape, 0)) + q
            done[s, q] = jnp.where(degree <= TRUNC, summed, 0.0).astype(bf16)
            store = pltpu.make_async_copy(done.at[s, q], out.at[s, q], sems.at[s, q])
            store.start()
            stores.append(store)
    for store in stores:
        store.wait()


def legendre_sum(wave_table, folded, other, first_table, second_table):
    slots, parities, pairs, _ = folded.shape
    degree_rows = first_table.shape[0]
    return pl.pallas_call(
        legendre_kernel,
        out_shape=jax.ShapeDtypeStruct((slots, parities, degree_rows, 128), bf16),
        in_specs=[pl.BlockSpec(memory_space=pltpu.VMEM)] * 5,
        out_specs=pl.BlockSpec(memory_space=pl.ANY),
        scratch_shapes=[
            pltpu.VMEM((slots * pairs, 128), f32),
            pltpu.VMEM((slots, parities, pairs, 128), bf16),
            pltpu.VMEM((slots, parities, degree_rows, 128), bf16),
            pltpu.SemaphoreType.DMA((slots, parities)),
        ],
        compiler_params=pltpu.CompilerParams(vmem_limit_bytes=LEGENDRE_VMEM),
        name="legendre",
    )(wave_table.reshape(1, 128), folded, other, first_table, second_table)


def on_device(grid_values, lat_counts, wave_table, inverses, legendre):
    pair_total = lat_counts.shape[0]
    slab_width = grid_values.shape[1]
    grouped = grid_values.reshape(pair_total, 2 * slab_width, grid_values.shape[2])
    swap = [(0, 1), (1, 0)]
    own = fourier(grouped, lat_counts, wave_table)
    other = lax.ppermute(own, "lev", swap)
    half = lax.dynamic_slice_in_dim(inverses, lax.axis_index("lev") * 16, 16, 2)
    half = half.astype(bf16).transpose(0, 2, 1, 3).reshape(2 * pair_total * 32, 32)
    matrices, first_table = fold_matrices(half, legendre)
    send = mix(matrices, own, other)
    slab = lax.all_to_all(
        send.reshape(64, 40, 128), "lat", split_axis=0, concat_axis=0, tiled=True
    )
    rest = lax.ppermute(slab, "lev", swap)
    folded, second_table = prepare(slab.reshape(2560, 128), legendre)
    return legendre_sum(
        wave_table, folded, rest.reshape(2560, 128), first_table, second_table
    )


def solution(mesh):
    placed = (
        P("lat", "lev", None),
        P("lat"),
        P(),
        P("lat", None, None, None),
        P("lat", None, "lev", None),
    )
    return jax.shard_map(
        on_device,
        mesh=mesh,
        in_specs=placed,
        out_specs=P("lat", None, "lev", None),
        check_vma=False,
    )
```
